128 devices in a mesh: pipe: 8 (over z_lo, x), ctx: 8 (over y, core), tp: 2 (over z_hi).
Axes of the slice: x: 4, y: 4, z: 4 (z_hi: 2, z_lo: 2; z = z_hi * 2 + z_lo), core: 2. Of those that a mesh axis runs over, the one named last changes fastest.
Arguments:
- queries: bfloat16 [8, 2048, 8192], P('pipe', 'ctx', 'tp'), may hold values from -16 to 16
- key_codes: bfloat16 [8, 2048, 512], P('pipe', 'ctx', 'tp'), may hold values from -127 to 127
- value_codes: bfloat16 [8, 2048, 512], P('pipe', 'ctx', 'tp'), may hold values from -127 to 127
- kv_scales: float32 [8, 16, 8], P('pipe', 'ctx'), may hold values from 0.004 to 0.032
- saved_out: bfloat16 [8, 2048, 8192], P('pipe', 'ctx', 'tp'), may hold values from -6 to 6
- section_grads: bfloat16 [8, 2048, 8192], P('pipe', 'ctx', 'tp'), may hold values from -6 to 6
- block_order: int32 [16], replicated, may hold values from 0 to 15, as said below
- block_docs: int32 [16], replicated, may hold values from 0 to 2, never falling along the last dimension, each value on 1 to 9 neighbouring positions
Outputs:
- grad_queries: bfloat16 [8, 2048, 8192], P('pipe', 'ctx', 'tp')
- grad_keys: bfloat16 [8, 2048, 512], P('pipe', ('ctx', 'tp'))
- grad_values: bfloat16 [8, 2048, 512], P('pipe', ('ctx', 'tp'))
The draws below stay inside these ranges and needn't reach their ends.
Inputs may be any that keep to these rules, and one draw needn't show every extreme that they name: `block_order`: a permutation of the 16 sequence blocks; stored blocks 2 d and 2 d + 1 are sequence blocks p and 15 - p for some p.
All inputs are finite; a program needn't handle non-finite values.
Results may differ from the reference program's by a relative error of at most 0.0072.
Values may be sent and summed in bfloat16 or wider, within the bound.
No kernel may reach another device: no remote copies, remote signals or barrier semaphores. Data moves between devices by JAX's collectives and lax.ppermute only.
A program may use at most 192 MiB of HBM per device.

```python
import math
import jax
import jax.numpy as jnp
import numpy as np
from jax import lax

HQ = 64
KVH = 4
HD = 128
SECTIONS = 8
TOKENS = 2048
NB = 16
BLK = 128


def code_table(key, tie):
    shape = (SECTIONS, TOKENS, KVH * HD)
    codes = jax.random.randint(key, shape, -127, 128).astype(jnp.float32)
    rows = jnp.arange(TOKENS)
    target_rows = rows % BLK == BLK // 2 - 1
    columns = jnp.arange(KVH * HD)
    kept_column = columns % HD != HD - 1
    following = jnp.roll(codes, -1, axis=1)
    copy_here = target_rows[None, :, None] & kept_column[None, None, :] & (tie > 0.5)
    return jnp.where(copy_here, following, codes)


def draw_key_codes(key, part):
    codes = code_table(key, 0.0)
    return codes.astype(jnp.bfloat16)


def draw_queries(key, part):
    shape = (SECTIONS, TOKENS, HQ * HD)
    key = jax.random.fold_in(key, 3)
    values = jnp.clip(jax.random.normal(key, shape, jnp.float32), -6.0, 6.0)
    return values.astype(jnp.bfloat16)


def draw_value_codes(key, part):
    key = jax.random.fold_in(key, 7)
    codes = jax.random.randint(key, (SECTIONS, TOKENS, KVH * HD), -127, 128)
    return codes.astype(jnp.float32).astype(jnp.bfloat16)


def draw_kv_scales(key, part):
    key = jax.random.fold_in(key, 5)
    shape = (SECTIONS, NB, 2 * KVH)
    spread = jax.random.uniform(key, shape, jnp.float32, jnp.log(0.004), jnp.log(0.032))
    scales = jnp.exp(spread)
    return scales


def draw_block_order(key, part):
    key = jax.random.fold_in(key, 11)
    pairs = NB // 2
    chosen = jax.random.permutation(key, pairs).astype(jnp.int32)
    partner = (NB - 1 - chosen).astype(jnp.int32)
    return jnp.stack([chosen, partner], axis=1).reshape(NB)


def steps_of(rng, shape, shards, least, largest):
    factor_of = 1.0
    for axis_at, blocks in shards:
        draws = jax.random.uniform(jax.random.fold_in(jax.random.fold_in(rng, 6), axis_at), (blocks,), jnp.float32, least / len(shards), largest / len(shards))
        factor_of = factor_of * jnp.repeat(jnp.exp(draws), shape[axis_at] // blocks).reshape((-1,) + (1,) * (len(shape) - 1 - axis_at))
    return factor_of


def profile(count, total, bound, lean):
    weights = [(1 << 20) // math.isqrt(standing ** lean) + 1 for standing in range(2, count + 1)]
    surplus, given = total - bound - (count - 1), [1] * (count - 1)
    while surplus > 0:
        free = [i for i in range(count - 1) if given[i] < bound]
        mass, budget = sum([weights[i] for i in free]), surplus
        for i in free:
            addition = min(bound - given[i], max(1, budget * weights[i] // mass), surplus)
            given[i] = given[i] + addition
            surplus = surplus - addition
    return np.array([bound] + given)


def uneven(key, amount, total, reach, lean):
    if amount == 2:
        one = jax.random.randint(key, (), max(1, total - reach), min(reach, total - 1) + 1)
        return jnp.stack([one, total - one])
    lengths = jnp.asarray(profile(amount, total, reach, lean), jnp.int32)
    pairs = (amount - 1) // 2
    giver, taker = lengths[1:1 + 2 * pairs:2], lengths[2:2 + 2 * pairs:2]
    slack = jnp.minimum(giver - 1, reach - taker)
    shifted = jax.random.randint(jax.random.fold_in(key, 1), (pairs,), 0, 1 << 20) % (slack + 1)
    lengths = lengths.at[1:1 + 2 * pairs:2].set(giver - shifted).at[2:2 + 2 * pairs:2].set(taker + shifted)
    return lengths[jax.random.permutation(jax.random.fold_in(key, 2), amount)]


def noise(key, shape, scale, bound, shards=(), kind=jnp.bfloat16):
    values = scale * jax.random.normal(key, shape, jnp.float32)
    if shards:
        values = values * steps_of(key, shape, shards, -0.22, 0.18)
    return jnp.clip(values, -bound, bound).astype(kind)


def setup_inputs(seed: int = 0) -> dict:
    key_of = jax.random.split(jax.random.key(seed), 9)
    return {
        "queries": draw_queries(jax.random.fold_in(key_of[8], 71), 0),
        "key_codes": draw_key_codes(jax.random.fold_in(key_of[8], 71), 0),
        "value_codes": draw_value_codes(jax.random.fold_in(key_of[8], 71), 0),
        "kv_scales": draw_kv_scales(jax.random.fold_in(key_of[8], 71), 0),
        "saved_out": noise(key_of[4], (SECTIONS, TOKENS, HQ * HD), 1.0, 6.0, ((0, 8), (1, 8), (2, 2))),
        "section_grads": noise(key_of[5], (SECTIONS, TOKENS, HQ * HD), 1.0, 6.0, ((0, 8), (1, 8), (2, 2))),
        "block_order": draw_block_order(jax.random.fold_in(key_of[8], 71), 0),
        "block_docs": jnp.searchsorted(jnp.cumsum(uneven(key_of[7], 3, NB, NB // 2 + 1, 1)), jnp.arange(NB), side="right").astype(jnp.int32),
    }


masked_floor = -1.0e30


def section_backward(queries, key_codes, value_codes, scales, forward_out, grad_out, seq_blocks, positions, block_docs):
    inverse = HD ** -0.5
    repeats = HQ // KVH
    key_scale = jnp.repeat(scales[:, :KVH], BLK, axis=0)
    value_scale = jnp.repeat(scales[:, KVH:], BLK, axis=0)
    keys = (key_codes.astype(jnp.float32).reshape(TOKENS, KVH, HD) * key_scale[:, :, None]).astype(jnp.bfloat16)
    values = (value_codes.astype(jnp.float32).reshape(TOKENS, KVH, HD) * value_scale[:, :, None]).astype(jnp.bfloat16)
    documents = block_docs[seq_blocks]
    visible = (positions[None, :] <= positions[:, None]) & (documents[None, :] == documents[:, None])
    query_all = queries.reshape(TOKENS, KVH, repeats, HD)
    grad_all = grad_out.reshape(TOKENS, KVH, repeats, HD)
    out_all = forward_out.reshape(TOKENS, KVH, repeats, HD)
    highest = lax.Precision.HIGHEST

    def one_group(group):
        query = lax.dynamic_index_in_dim(query_all, group, 1, keepdims=False).astype(jnp.float32)
        grad_here = lax.dynamic_index_in_dim(grad_all, group, 1, keepdims=False).astype(jnp.float32)
        out_here = lax.dynamic_index_in_dim(out_all, group, 1, keepdims=False).astype(jnp.float32)
        key_here = lax.dynamic_index_in_dim(keys, group, 1, keepdims=False).astype(jnp.float32)
        value_here = lax.dynamic_index_in_dim(values, group, 1, keepdims=False).astype(jnp.float32)
        scores = jnp.einsum('ird,jd->rij', query, key_here, precision=highest) * inverse
        running_max = jnp.max(jnp.where(visible[None], scores, masked_floor), axis=-1)
        running_sum = jnp.sum(jnp.where(visible[None], jnp.exp(scores - running_max[..., None]), 0.0), axis=-1)
        log_norm = running_max + jnp.log(running_sum)
        probs = jnp.where(visible[None], jnp.exp(scores - log_norm[..., None]), 0.0)
        row_dots = jnp.transpose(jnp.sum(grad_here * out_here, axis=-1))
        dprobs = jnp.einsum('ird,jd->rij', grad_here, value_here, precision=highest)
        dscores = (probs * (dprobs - row_dots[:, :, None]) * inverse).astype(jnp.bfloat16)
        dscores = lax.optimization_barrier(dscores).astype(jnp.float32)
        probs_low = lax.optimization_barrier(probs.astype(jnp.bfloat16)).astype(jnp.float32)
        grad_query = jnp.einsum('rij,jd->ird', dscores, key_here, precision=highest)
        grad_key = jnp.einsum('rij,ird->jd', dscores, query, precision=highest)
        grad_value = jnp.einsum('rij,ird->jd', probs_low, grad_here, precision=highest)
        return grad_query, grad_key, grad_value

    grad_query, grad_key, grad_value = lax.map(one_group, jnp.arange(KVH, dtype=jnp.int32))
    grad_query = jnp.transpose(grad_query, (1, 0, 2, 3)).reshape(TOKENS, HQ * HD).astype(jnp.bfloat16)
    grad_key = jnp.transpose(grad_key, (1, 0, 2)).reshape(TOKENS, KVH * HD).astype(jnp.bfloat16)
    grad_value = jnp.transpose(grad_value, (1, 0, 2)).reshape(TOKENS, KVH * HD).astype(jnp.bfloat16)
    return grad_query, grad_key, grad_value


def reference(queries, key_codes, value_codes, kv_scales, saved_out, section_grads, block_order, block_docs):
    rows = jnp.arange(TOKENS, dtype=jnp.int32)
    seq_blocks = block_order[rows // BLK].astype(jnp.int32)
    positions = seq_blocks * BLK + rows % BLK
    incoming = jnp.roll(section_grads, -1, axis=0)
    query_list = []
    key_list = []
    value_list = []
    for section in range(SECTIONS):
        grad_query, grad_key, grad_value = section_backward(queries[section], key_codes[section], value_codes[section], kv_scales[section], saved_out[section], incoming[section], seq_blocks, positions, block_docs)
        query_list.append(grad_query)
        key_list.append(grad_key)
        value_list.append(grad_value)
    return jnp.stack(query_list), jnp.stack(key_list), jnp.stack(value_list)
```

```python
import functools
import math

import jax
import jax.numpy as jnp
from jax import lax
from jax.experimental import pallas as pl
from jax.experimental.pallas import tpu as pltpu
from jax.sharding import PartitionSpec as P

HQ = 64
KVH = 4
HD = 128
BLK = 128
BLOCKS = 16
TOKENS = BLOCKS * BLK
LONGEST = 9
INVERSE = HD**-0.5
INVERSE2 = INVERSE * math.log2(math.e)
NT = (((1,), (1,)), ((), ()))
F32 = jnp.float32
BF16 = jnp.bfloat16

CHUNKS = ((0, 2048), (2048, 1024), (3072, 1024))
GROUP = HQ // KVH * HD
STEP = 512
SMEM = pl.BlockSpec(memory_space=pltpu.SMEM)
VMEM = pl.BlockSpec(memory_space=pltpu.VMEM)


def turned(array, axis, by):
    size = lax.axis_size(axis)
    return lax.ppermute(array, axis, [(i, (i + by) % size) for i in range(size)])


def core_swap(array):
    size = lax.axis_size("ctx")
    return lax.ppermute(array, "ctx", [(i, i ^ 1) for i in range(size)])


def stacked(tile):
    heads = tile.shape[1] // HD
    return jnp.concatenate([tile[:, i * HD : (i + 1) * HD] for i in range(heads)], axis=0)


def dequantize_kernel(place_ref, key_ref, value_ref, scale_ref, out_ref):
    head = place_ref[2] * 2
    for block in range(2):
        rows = slice(block * BLK, (block + 1) * BLK)
        for part, codes in enumerate((key_ref, value_ref)):
            for g in range(2):
                scale = scale_ref[block, part * KVH + head + g]
                tile = codes[rows, g * HD : (g + 1) * HD].astype(F32) * scale
                at = (part * 2 + g) * HD
                out_ref[rows, at : at + HD] = tile.astype(BF16)


def order_kernel(place_ref, order_ref, *refs):
    pieces = (refs[:4], refs[4:8])
    keys_ref, turned_ref, values_ref = refs[8:]
    y = place_ref[0]
    core = place_ref[1]
    for d in range(4):
        from_y = lax.rem(y + 4 - d, 4)
        for which in range(2):
            holder = core if which == 0 else 1 - core
            for block in range(2):
                seq = order_ref[from_y * 4 + holder * 2 + block]
                at = pl.multiple_of(seq * BLK, BLK)
                rows = slice(block * BLK, (block + 1) * BLK)
                tile = pieces[which][d][rows, :]
                for g in range(2):
                    key = tile[:, g * HD : (g + 1) * HD]
                    keys_ref[g, pl.ds(at, BLK), :] = key
                    turned_ref[g, :, pl.ds(at, BLK)] = jnp.transpose(key)
                    values_ref[g, pl.ds(at, BLK), :] = tile[:, (2 + g) * HD : (3 + g) * HD]


def block_pairs(size, start, key_ref, turned_ref, value_ref, q_ref, g_ref, o_ref, dq_ref, dk_ref, dv_ref):
    rows = size * BLK
    first = pl.multiple_of(start * BLK, BLK)
    keys = key_ref[0, pl.ds(first, rows), :]
    values = value_ref[0, pl.ds(first, rows), :]
    keys_turned = turned_ref[0, :, pl.ds(first, rows)]
    lane = lax.broadcasted_iota(jnp.int32, (BLK, HD), 1)
    dots = jnp.zeros((BLK, HD), F32)
    for h in range(STEP // HD):
        columns = slice(h * HD, (h + 1) * HD)
        product = g_ref[:, columns].astype(F32) * o_ref[:, columns].astype(F32)
        dots = jnp.where(lane == h, jnp.sum(product, axis=1, keepdims=True), dots)
    dots = jnp.transpose(dots)
    wide = 2 * HD
    key_index = lax.broadcasted_iota(jnp.int32, (BLK, wide), 0)
    query_index = lax.broadcasted_iota(jnp.int32, (BLK, wide), 1) % BLK
    dk = None
    dv = None
    for part in range(STEP // wide):
        columns = slice(part * wide, (part + 1) * wide)
        query = stacked(q_ref[:, columns])
        grad = stacked(g_ref[:, columns])
        scores = lax.dot_general(keys, query, NT, preferred_element_type=F32)
        dprobs = lax.dot_general(values, grad, NT, preferred_element_type=F32)
        row_dots = jnp.concatenate([dots[part * 2 + i : part * 2 + i + 1] for i in range(2)], axis=1)
        last = jnp.where(key_index <= query_index, scores[rows - BLK :], -jnp.inf)
        scores = last if size == 1 else jnp.concatenate([scores[: rows - BLK], last], axis=0)
        top = jnp.max(scores, axis=0, keepdims=True)
        weights = jnp.exp2((scores - top) * INVERSE2)
        total = jnp.sum(weights, axis=0, keepdims=True)
        probs = weights * (1.0 / total)
        dscores = (probs * (dprobs - row_dots)).astype(BF16)
        dv_part = jnp.dot(probs.astype(BF16), grad, preferred_element_type=F32)
        dk_part = jnp.dot(dscores, query, preferred_element_type=F32)
        dv = dv_part if dv is None else dv + dv_part
        dk = dk_part if dk is None else dk + dk_part
        dq = jnp.dot(keys_turned, dscores, preferred_element_type=F32) * INVERSE
        for i in range(2):
            at = part * wide + i * HD
            dq_ref[:, at : at + HD] = jnp.transpose(dq[:, i * HD : (i + 1) * HD]).astype(BF16)
    dv_ref[pl.ds(first, rows), :] += dv
    dk_ref[pl.ds(first, rows), :] += dk


def chunk_kernel(opens, closes, aliased, place_ref, order_ref, docs_ref, key_ref, turned_ref, value_ref, q_ref, g_ref, o_ref, *refs):
    refs = list(refs)
    sums_in = None if opens else refs.pop(0)
    if aliased:
        refs.pop(0)
    dq_ref = refs.pop(0)
    *out_refs, sums_ref = refs
    step = pl.program_id(0)
    half = pl.program_id(1)

    @pl.when((step == 0) & (half == 0))
    def _():
        sums_ref[...] = jnp.zeros_like(sums_ref) if opens else sums_in[...]

    seq = order_ref[place_ref[0] * 4 + place_ref[1] * 2 + half]
    doc = docs_ref[seq]
    start = jnp.int32(0)
    for b in range(BLOCKS):
        start = start + jnp.where(docs_ref[b] < doc, 1, 0)
    size = seq + 1 - start
    for i in range(1, LONGEST + 1):

        @pl.when(size == i)
        def _():
            block_pairs(
                i, start, key_ref, turned_ref, value_ref, q_ref, g_ref, o_ref, dq_ref, sums_ref.at[0], sums_ref.at[1]
            )

    if closes:

        @pl.when((step == pl.num_programs(0) - 1) & (half == 1))
        def _():
            for block in range(2):
                rows = slice(block * BLK, (block + 1) * BLK)
                for y in range(4):
                    for which in range(2):
                        core = place_ref[1] if which == 0 else 1 - place_ref[1]
                        at = pl.multiple_of(order_ref[y * 4 + core * 2 + block] * BLK, BLK)
                        out_refs[which * 2][y, rows, :] = (sums_ref[0, pl.ds(at, BLK), :] * INVERSE).astype(BF16)
                        out_refs[which * 2 + 1][y, rows, :] = sums_ref[1, pl.ds(at, BLK), :].astype(BF16)


def chunk_call(chunk, place, order, docs, keys, turned_keys, values, queries, grad, saved, sums, dq):
    first, width = chunk
    group = first // GROUP
    opens = first % GROUP == 0
    closes = (first + width) % GROUP == 0
    offset = first // STEP
    head = lambda s: pl.BlockSpec((1,) + s, lambda i, j, *_: (group, 0, 0))
    columns = pl.BlockSpec((BLK, STEP), lambda i, j, *_: (j, i + offset))
    own_columns = pl.BlockSpec((BLK, STEP), lambda i, j, *_: (j, i))
    whole = lambda s: pl.BlockSpec(s, lambda i, j, *_: (0,) * len(s))
    sums_shape = (2, TOKENS, HD)
    in_specs = [head((TOKENS, HD)), head((HD, TOKENS)), head((TOKENS, HD)), columns, own_columns, columns]
    operands = [keys, turned_keys, values, queries, grad, saved]
    if not opens:
        in_specs.append(whole(sums_shape))
        operands.append(sums)
    aliases = {}
    if dq is not None:
        aliases = {3 + len(operands): 0}
        in_specs.append(pl.BlockSpec(memory_space=pl.ANY))
        operands.append(dq)
    out_specs = [columns]
    out_shape = [jax.ShapeDtypeStruct(queries.shape, BF16)]
    scratch = []
    if closes:
        pieces = [jax.ShapeDtypeStruct((4, 2 * BLK, HD), BF16)] * 4
        out_specs += [whole(piece.shape) for piece in pieces]
        out_shape += pieces
        scratch = [pltpu.VMEM(sums_shape, F32)]
    else:
        out_specs.append(whole(sums_shape))
        out_shape.append(jax.ShapeDtypeStruct(sums_shape, F32))
    return pl.pallas_call(
        functools.partial(chunk_kernel, opens, closes, dq is not None),
        grid_spec=pltpu.PrefetchScalarGridSpec(
            num_scalar_prefetch=3,
            grid=(width // STEP, 2),
            in_specs=in_specs,
            out_specs=out_specs,
            scratch_shapes=scratch,
        ),
        out_shape=out_shape,
        input_output_aliases=aliases,
        compiler_params=pltpu.CompilerParams(vmem_limit_bytes=48 << 20),
        cost_estimate=TINY,
    )(place, order, docs, *operands)


def pair_kernel(place_ref, *refs):
    for d in range(4):
        y = lax.rem(place_ref[0] + d, 4)
        for part in range(2):
            columns = slice(part * HD, (part + 1) * HD)
            total = refs[part][y].astype(F32) + refs[2 + part][y].astype(F32)
            refs[4 + d][:, columns] = total.astype(refs[4 + d].dtype)


def chips_kernel(place_ref, *refs):
    groups = (refs[:4], refs[4:8])
    for out_ref, block in ((refs[8], place_ref[2]), (refs[9], 1 - place_ref[2])):
        rows = pl.ds(pl.multiple_of(block * BLK, BLK), BLK)
        for g, sums in enumerate(groups):
            total = sums[0][rows, :]
            for ref in sums[1:]:
                total = total + ref[rows, :].astype(F32)
            out_ref[:, g * 2 * HD : (g + 1) * 2 * HD] = total.astype(BF16)


def join_kernel(place_ref, keep_ref, sent_ref, *out_refs):
    for tp in range(2):
        for g in range(2):
            at = (tp * 2 + g) * HD
            for part in range(2):
                columns = slice((g * 2 + part) * HD, (g * 2 + part + 1) * HD)
                kept = keep_ref[:, columns].astype(F32)
                sent = sent_ref[:, columns].astype(F32)
                out_refs[part][:, at : at + HD] = jnp.where(place_ref[2] == tp, kept, sent).astype(BF16)


def tied(array, *others):
    return lax.optimization_barrier((array,) + others)[0]


TINY = pl.CostEstimate(flops=1_000_000, bytes_accessed=100_000, transcendentals=0)


def pair_sum(place, mine, arrived):
    piece = (2 * BLK, 2 * HD)
    own, *further = pl.pallas_call(
        pair_kernel,
        in_specs=[SMEM] + [VMEM] * 4,
        out_specs=[VMEM] * 4,
        out_shape=[jax.ShapeDtypeStruct(piece, F32)] + [jax.ShapeDtypeStruct(piece, BF16)] * 3,
        cost_estimate=TINY,
    )(place, *mine, *arrived)
    return own, further


def between_chips(further):
    return [turned(further[d - 1], "ctx", 2 * d) for d in range(1, 4)]


def on_device(queries, key_codes, value_codes, kv_scales, saved_out, section_grads, block_order, block_docs):
    pieces = [section_grads[0, :, first : first + width] for first, width in CHUNKS]
    incoming = [turned(pieces[0], "pipe", -1), turned(pieces[1], "pipe", -1)]
    incoming.append(turned(tied(pieces[2], incoming[0]), "pipe", -1))
    ctx = lax.axis_index("ctx")
    place = jnp.stack([ctx // 2, ctx % 2, lax.axis_index("tp")]).astype(jnp.int32)

    pair = pl.pallas_call(
        dequantize_kernel,
        in_specs=[SMEM, VMEM, VMEM, SMEM],
        out_specs=VMEM,
        out_shape=jax.ShapeDtypeStruct((2 * BLK, 4 * HD), BF16),
        cost_estimate=TINY,
    )(place, key_codes[0], value_codes[0], kv_scales[0])
    mine = [pair] + [turned(pair, "ctx", 2 * d) for d in range(1, 4)]
    other = [core_swap(piece) for piece in mine]
    keys, turned_keys, values = pl.pallas_call(
        order_kernel,
        in_specs=[SMEM, SMEM] + [VMEM] * 8,
        out_specs=[VMEM] * 3,
        out_shape=[
            jax.ShapeDtypeStruct((2, TOKENS, HD), BF16),
            jax.ShapeDtypeStruct((2, HD, TOKENS), BF16),
            jax.ShapeDtypeStruct((2, TOKENS, HD), BF16),
        ],
        compiler_params=pltpu.CompilerParams(vmem_limit_bytes=32 << 20),
        cost_estimate=TINY,
    )(place, block_order, *mine, *other)

    shared = (place, block_order, block_docs, keys, turned_keys, values, queries[0])
    dq, *parts0 = chunk_call(CHUNKS[0], *shared, incoming[0], saved_out[0], None, None)
    arrived0 = [core_swap(tied(part, incoming[1])) for part in parts0[2:]]
    dq, sums = chunk_call(CHUNKS[1], *shared, incoming[1], saved_out[0], None, dq)
    own0, further0 = pair_sum(place, parts0[:2], [tied(part, sums) for part in arrived0])
    sums0 = [own0] + between_chips(further0)
    grad2 = tied(incoming[2], own0)
    dq, *parts1 = chunk_call(CHUNKS[2], *shared, grad2, saved_out[0], sums, dq)
    own1, further1 = pair_sum(place, parts1[:2], [core_swap(tied(part, *sums0)) for part in parts1[2:]])
    sums1 = [own1] + between_chips(further1)
    half = jax.ShapeDtypeStruct((BLK, 4 * HD), BF16)
    keep, send = pl.pallas_call(
        chips_kernel, in_specs=[SMEM] + [VMEM] * 8, out_specs=[VMEM] * 2, out_shape=[half] * 2, cost_estimate=TINY
    )(place, *sums0, *sums1)
    out = jax.ShapeDtypeStruct((BLK, KVH * HD), BF16)
    grad_keys, grad_values = pl.pallas_call(
        join_kernel, in_specs=[SMEM] + [VMEM] * 2, out_specs=[VMEM] * 2, out_shape=[out] * 2, cost_estimate=TINY
    )(place, keep, turned(send, "tp", 1))
    return dq[None], grad_keys[None], grad_values[None]


def solution(mesh):
    in_specs = (
        P("pipe", "ctx", "tp"),
        P("pipe", "ctx", "tp"),
        P("pipe", "ctx", "tp"),
        P("pipe", "ctx", None),
        P("pipe", "ctx", "tp"),
        P("pipe", "ctx", "tp"),
        P(),
        P(),
    )
    out_specs = (
        P("pipe", "ctx", "tp"),
        P("pipe", ("ctx", "tp"), None),
        P("pipe", ("ctx", "tp"), None),
    )
    return jax.shard_map(on_device, mesh=mesh, in_specs=in_specs, out_specs=out_specs, check_vma=False)
```

```python
import functools
import math

import jax
import jax.numpy as jnp
from jax import lax
from jax.experimental import pallas as pl
from jax.experimental.pallas import tpu as pltpu
from jax.sharding import PartitionSpec as P

HQ = 64
KVH = 4
HD = 128
BLK = 128
BLOCKS = 16
TOKENS = BLOCKS * BLK
ROWS = 2 * BLK
LONGEST = 9
INVERSE = HD**-0.5
INVERSE2 = INVERSE * math.log2(math.e)
NT = (((1,), (1,)), ((), ()))
F32 = jnp.float32
BF16 = jnp.bfloat16

GROUP = HQ // KVH * HD
STEP = 512
STEPS = GROUP // STEP
SMEM = pl.BlockSpec(memory_space=pltpu.SMEM)
VMEM = pl.BlockSpec(memory_space=pltpu.VMEM)
ANY = pl.BlockSpec(memory_space=pl.ANY)
TINY = pl.CostEstimate(flops=1_000_000, bytes_accessed=100_000, transcendentals=0)


def shape(*dims, dtype=BF16):
    return jax.ShapeDtypeStruct(dims, dtype)


def chip_turned(array, by):
    size = lax.axis_size("ctx")
    return lax.ppermute(array, "ctx", [(i, (i + 2 * by) % size) for i in range(size)])


def core_swap(array):
    size = lax.axis_size("ctx")
    return lax.ppermute(array, "ctx", [(i, i ^ 1) for i in range(size)])


def from_next_section(array, flip):
    sections, size = lax.axis_size("pipe"), lax.axis_size("ctx")
    moves = [
        (s * size + i, (s - 1) % sections * size + (i ^ flip)) for s in range(sections) for i in range(size)
    ]
    return lax.ppermute(array, ("pipe", "ctx"), moves)


def tied(array, *others):
    return lax.optimization_barrier((array,) + others)[0]


def dequantize_kernel(place_ref, key_ref, value_ref, scale_ref, keep_ref, send_ref):
    core = place_ref[1]
    for g in range(2):
        for block in range(2):
            rows = slice(block * BLK, (block + 1) * BLK)
            for part, codes in enumerate((key_ref, value_ref)):
                scale = scale_ref[block, part * KVH + place_ref[2] * 2 + g]
                tile = (codes[rows, g * HD : (g + 1) * HD].astype(F32) * scale).astype(BF16)

                @pl.when(core == g)
                def _():
                    keep_ref[rows, part * HD : (part + 1) * HD] = tile

                @pl.when(core != g)
                def _():
                    send_ref[rows, part * HD : (part + 1) * HD] = tile


def order_kernel(place_ref, order_ref, *refs):
    pieces = refs[:4]
    keys_ref, turned_ref, values_ref = refs[4:]
    y = place_ref[0]
    for d in range(4):
        from_y = lax.rem(y + 4 - d, 4)
        for half in range(2):
            holder = jnp.where(half == 0, place_ref[1], 1 - place_ref[1])
            for block in range(2):
                seq = order_ref[from_y * 4 + holder * 2 + block]
                at = pl.multiple_of(seq * BLK, BLK)
                tile = pieces[d][half, block * BLK : (block + 1) * BLK, :]
                keys_ref[pl.ds(at, BLK), :] = tile[:, :HD]
                turned_ref[:, pl.ds(at, BLK)] = jnp.transpose(tile[:, :HD])
                values_ref[pl.ds(at, BLK), :] = tile[:, HD:]


def stacked(tile):
    heads = tile.shape[1] // HD
    return jnp.concatenate([tile[:, i * HD : (i + 1) * HD] for i in range(heads)], axis=0)


def load_rows(query_from, grad_from, saved_from, q_ref, g_ref, dots_ref):
    lane = lax.broadcasted_iota(jnp.int32, (BLK, HD), 1)
    dots = jnp.zeros((BLK, HD), F32)
    for h in range(STEP // HD):
        columns = slice(h * HD, (h + 1) * HD)
        rows = slice(h * BLK, (h + 1) * BLK)
        grad = grad_from[:, columns]
        q_ref[rows, :] = query_from[:, columns]
        g_ref[rows, :] = grad
        product = grad.astype(F32) * saved_from[:, columns].astype(F32)
        dots = jnp.where(lane == h, jnp.sum(product, axis=1, keepdims=True), dots)
    dots_ref[...] = jnp.transpose(dots)


def block_pairs(size, start, key_ref, turned_ref, value_ref, q_ref, g_ref, dots_ref, dq_ref, dk_ref, dv_ref):
    rows = size * BLK
    first = pl.multiple_of(start * BLK, BLK)
    keys = key_ref[pl.ds(first, rows), :]
    values = value_ref[pl.ds(first, rows), :]
    keys_turned = turned_ref[:, pl.ds(first, rows)]
    wide = 2 * HD
    key_index = lax.broadcasted_iota(jnp.int32, (BLK, wide), 0)
    query_index = lax.broadcasted_iota(jnp.int32, (BLK, wide), 1) % BLK
    dk = None
    dv = None
    for part in range(STEP // wide):
        query = q_ref[part * wide : (part + 1) * wide, :]
        grad = g_ref[part * wide : (part + 1) * wide, :]
        scores = lax.dot_general(keys, query, NT, preferred_element_type=F32)
        dprobs = lax.dot_general(values, grad, NT, preferred_element_type=F32)
        row_dots = jnp.concatenate([dots_ref[part * 2 + i : part * 2 + i + 1, :] for i in range(2)], axis=1)
        last = jnp.where(key_index <= query_index, scores[rows - BLK :], -jnp.inf)
        scores = last if size == 1 else jnp.concatenate([scores[: rows - BLK], last], axis=0)
        top = jnp.max(scores, axis=0, keepdims=True)
        weights = jnp.exp2((scores - top) * INVERSE2)
        total = jnp.sum(weights, axis=0, keepdims=True)
        probs = weights * (1.0 / total)
        dscores = (probs * (dprobs - row_dots)).astype(BF16)
        dv_part = jnp.dot(probs.astype(BF16), grad, preferred_element_type=F32)
        dk_part = jnp.dot(dscores, query, preferred_element_type=F32)
        dv = dv_part if dv is None else dv + dv_part
        dk = dk_part if dk is None else dk + dk_part
        dq = jnp.dot(keys_turned, dscores, preferred_element_type=F32) * INVERSE
        for i in range(2):
            at = part * wide + i * HD
            dq_ref[:, at : at + HD] = jnp.transpose(dq[:, i * HD : (i + 1) * HD]).astype(BF16)
    dv_ref[pl.ds(first, rows), :] += dv
    dk_ref[pl.ds(first, rows), :] += dk


def rows_kernel(rows_of, place_ref, order_ref, docs_ref, key_ref, turned_ref, value_ref, query_ref, grad_ref, saved_ref, *refs):
    refs = list(refs)
    before_ref = refs.pop(0) if rows_of else None
    dq_ref, out_ref, q_scr, g_scr, dots_scr, *rest = refs
    sums_ref = rest.pop(0) if rows_of else out_ref
    step = pl.program_id(0)
    block = pl.program_id(1)

    @pl.when((step == 0) & (block == 0))
    def _():
        if rows_of:
            pltpu.make_async_copy(before_ref, rest[0], rest[1]).start()
        sums_ref[...] = jnp.zeros_like(sums_ref)

    load_rows(query_ref, grad_ref, saved_ref, q_scr, g_scr, dots_scr)
    core = 1 - place_ref[1] if rows_of else place_ref[1]
    seq = order_ref[place_ref[0] * 4 + core * 2 + block]
    doc = docs_ref[seq]
    start = jnp.int32(0)
    for b in range(BLOCKS):
        start = start + jnp.where(docs_ref[b] < doc, 1, 0)
    size = seq + 1 - start
    for i in range(1, LONGEST + 1):

        @pl.when(size == i)
        def _():
            block_pairs(
                i, start, key_ref, turned_ref, value_ref, q_scr, g_scr, dots_scr, dq_ref, sums_ref.at[0], sums_ref.at[1]
            )

    if rows_of:

        @pl.when((step == STEPS - 1) & (block == 1))
        def _():
            pltpu.make_async_copy(before_ref, rest[0], rest[1]).wait()
            for r in range(BLOCKS):
                at = pl.ds(pl.multiple_of(order_ref[r] * BLK, BLK), BLK)
                out_ref[r, :, :HD] = ((sums_ref[0, at, :] + rest[0][0, at, :]) * INVERSE).astype(BF16)
                out_ref[r, :, HD:] = (sums_ref[1, at, :] + rest[0][1, at, :]).astype(BF16)


def rows_call(rows_of, place, order, docs, kv, queries, saved, grads, sums):
    whole = lambda s: pl.BlockSpec(s, lambda i, j, *_: (0,) * len(s))
    group_at = pl.BlockSpec((BLK, STEP), lambda i, j, p, *_: (j, p[1] * STEPS + i))
    alone_at = pl.BlockSpec((BLK, STEP), lambda i, j, *_: (j, i))
    sums_shape = (2, TOKENS, HD)
    in_specs = [whole((TOKENS, HD)), whole((HD, TOKENS)), whole((TOKENS, HD)), group_at, alone_at, group_at]
    operands = [*kv, queries, grads, saved]
    scratch = [pltpu.VMEM((STEP, HD), BF16), pltpu.VMEM((STEP, HD), BF16), pltpu.VMEM((HD, BLK), F32)]
    if rows_of:
        in_specs.append(ANY)
        operands.append(sums)
        outs = [shape(ROWS, GROUP), shape(BLOCKS, BLK, 2 * HD)]
        scratch += [pltpu.VMEM(sums_shape, F32), pltpu.VMEM(sums_shape, F32), pltpu.SemaphoreType.DMA]
    else:
        outs = [shape(*queries.shape), shape(*sums_shape, dtype=F32)]
    return pl.pallas_call(
        functools.partial(rows_kernel, rows_of),
        grid_spec=pltpu.PrefetchScalarGridSpec(
            num_scalar_prefetch=3,
            grid=(STEPS, 2),
            in_specs=in_specs,
            out_specs=[alone_at if rows_of else group_at, whole(outs[1].shape)],
            scratch_shapes=scratch,
        ),
        out_shape=outs,
        compiler_params=pltpu.CompilerParams(vmem_limit_bytes=62 << 20),
        cost_estimate=TINY,
    )(place, order, docs, *operands)


def total_kernel(parts_ref, keys_ref, values_ref):
    for core in range(2):
        for tp in range(2):
            at = (tp * 2 + core) * HD
            total = parts_ref[core * 2 + tp].astype(F32)
            for y in range(1, 4):
                total = total + parts_ref[y * 4 + core * 2 + tp].astype(F32)
            keys_ref[:, at : at + HD] = total[:, :HD].astype(BF16)
            values_ref[:, at : at + HD] = total[:, HD:].astype(BF16)


def place_kernel(place_ref, piece_ref, _, out_ref):
    out_ref[...] = piece_ref[...]


def on_device(queries, key_codes, value_codes, kv_scales, saved_out, section_grads, block_order, block_docs):
    ctx = lax.axis_index("ctx")
    core = ctx % 2
    place = jnp.stack([ctx // 2, core, lax.axis_index("tp")]).astype(jnp.int32)
    queries, saved_out, section_grads = queries[0], saved_out[0], section_grads[0]

    grads = []
    for flip in range(2):
        group = core if flip == 0 else 1 - core
        piece = lax.dynamic_slice_in_dim(section_grads, group * GROUP, GROUP, 1)
        grads.append(from_next_section(piece, flip))

    keep, send = pl.pallas_call(
        dequantize_kernel,
        in_specs=[SMEM, VMEM, VMEM, SMEM],
        out_specs=[VMEM] * 2,
        out_shape=[shape(ROWS, 2 * HD)] * 2,
        cost_estimate=TINY,
    )(place, key_codes[0], value_codes[0], kv_scales[0])
    sent = [core_swap(array) for array in (queries, saved_out)]
    chip = tied(jnp.stack([keep, core_swap(send)]), *sent)
    chips = [chip] + [chip_turned(chip, d) for d in range(1, 4)]
    kv = pl.pallas_call(
        order_kernel,
        in_specs=[SMEM, SMEM] + [VMEM] * 4,
        out_specs=[VMEM] * 3,
        out_shape=[shape(TOKENS, HD), shape(HD, TOKENS), shape(TOKENS, HD)],
        compiler_params=pltpu.CompilerParams(vmem_limit_bytes=62 << 20),
        cost_estimate=TINY,
    )(place, block_order, *chips)

    shared = (place, block_order, block_docs, kv)
    dq, sums = rows_call(0, *shared, queries, saved_out, grads[0], None)
    dq_other, sums = rows_call(1, *shared, *sent, grads[1], sums)
    returned = core_swap(dq_other)
    parts = lax.all_to_all(sums, ("ctx", "tp"), 0, 0, tiled=True)
    dq = pl.pallas_call(
        place_kernel,
        grid_spec=pltpu.PrefetchScalarGridSpec(
            num_scalar_prefetch=1,
            grid=(4,),
            in_specs=[pl.BlockSpec((BLK // 2, GROUP), lambda i, p: (i, 0)), ANY],
            out_specs=pl.BlockSpec((BLK // 2, GROUP), lambda i, p: (i, 1 - p[1])),
        ),
        out_shape=shape(*queries.shape),
        input_output_aliases={2: 0},
        cost_estimate=TINY,
    )(place, returned, dq)
    grad_keys, grad_values = pl.pallas_call(
        total_kernel,
        in_specs=[VMEM],
        out_specs=[VMEM] * 2,
        out_shape=[shape(BLK, KVH * HD)] * 2,
        compiler_params=pltpu.CompilerParams(vmem_limit_bytes=62 << 20),
        cost_estimate=TINY,
    )(tied(parts, dq))
    return dq[None], grad_keys[None], grad_values[None]


def solution(mesh):
    in_specs = (
        P("pipe", "ctx", "tp"),
        P("pipe", "ctx", "tp"),
        P("pipe", "ctx", "tp"),
        P("pipe", "ctx", None),
        P("pipe", "ctx", "tp"),
        P("pipe", "ctx", "tp"),
        P(),
        P(),
    )
    out_specs = (
        P("pipe", "ctx", "tp"),
        P("pipe", ("ctx", "tp"), None),
        P("pipe", ("ctx", "tp"), None),
    )
    return jax.shard_map(on_device, mesh=mesh, in_specs=in_specs, out_specs=out_specs, check_vma=False)
```

```python
import functools
import math

import jax
import jax.numpy as jnp
from jax import lax
from jax.experimental import pallas as pl
from jax.experimental.pallas import tpu as pltpu
from jax.sharding import PartitionSpec as P

HQ = 64
KVH = 4
HD = 128
BLK = 128
BLOCKS = 16
TOKENS = BLOCKS * BLK
ROWS = 2 * BLK
LONGEST = 9
INVERSE = HD**-0.5
INVERSE2 = INVERSE * math.log2(math.e)
NT = (((1,), (1,)), ((), ()))
F32 = jnp.float32
BF16 = jnp.bfloat16

GROUP = HQ // KVH * HD
STEP = 512
STEPS = GROUP // STEP
SMEM = pl.BlockSpec(memory_space=pltpu.SMEM)
VMEM = pl.BlockSpec(memory_space=pltpu.VMEM)
ANY = pl.BlockSpec(memory_space=pl.ANY)
TINY = pl.CostEstimate(flops=1_000_000, bytes_accessed=100_000, transcendentals=0)


def shape(*dims, dtype=BF16):
    return jax.ShapeDtypeStruct(dims, dtype)


def chip_turned(array, by):
    size = lax.axis_size("ctx")
    return lax.ppermute(array, "ctx", [(i, (i + 2 * by) % size) for i in range(size)])


def turned(array, axis):
    size = lax.axis_size(axis)
    return lax.ppermute(array, axis, [(i, (i + 1) % size) for i in range(size)])


def across(array):
    size = lax.axis_size("ctx")
    moves = [(i * 2 + t, (i ^ 1) * 2 + 1 - t) for i in range(size) for t in range(2)]
    return lax.ppermute(array, ("ctx", "tp"), moves)


def core_swap(array):
    size = lax.axis_size("ctx")
    return lax.ppermute(array, "ctx", [(i, i ^ 1) for i in range(size)])


def from_next_section(array, flip):
    sections, size = lax.axis_size("pipe"), lax.axis_size("ctx")
    moves = [
        (s * size + i, (s - 1) % sections * size + (i ^ flip)) for s in range(sections) for i in range(size)
    ]
    return lax.ppermute(array, ("pipe", "ctx"), moves)


def tied(array, *others):
    return lax.optimization_barrier((array,) + others)[0]


def dequantize_kernel(place_ref, key_ref, value_ref, scale_ref, keep_ref, send_ref):
    core = place_ref[1]
    for g in range(2):
        for block in range(2):
            rows = slice(block * BLK, (block + 1) * BLK)
            for part, codes in enumerate((key_ref, value_ref)):
                scale = scale_ref[block, part * KVH + place_ref[2] * 2 + g]
                tile = (codes[rows, g * HD : (g + 1) * HD].astype(F32) * scale).astype(BF16)

                @pl.when(core == g)
                def _():
                    keep_ref[rows, part * HD : (part + 1) * HD] = tile

                @pl.when(core != g)
                def _():
                    send_ref[rows, part * HD : (part + 1) * HD] = tile


def order_kernel(place_ref, order_ref, *refs):
    pieces = refs[:4]
    keys_ref, turned_ref, values_ref = refs[4:]
    y = place_ref[0]
    for d in range(4):
        from_y = lax.rem(y + 4 - d, 4)
        for half in range(2):
            holder = jnp.where(half == 0, place_ref[1], 1 - place_ref[1])
            for block in range(2):
                seq = order_ref[from_y * 4 + holder * 2 + block]
                at = pl.multiple_of(seq * BLK, BLK)
                tile = pieces[d][half, block * BLK : (block + 1) * BLK, :]
                keys_ref[pl.ds(at, BLK), :] = tile[:, :HD]
                turned_ref[:, pl.ds(at, BLK)] = jnp.transpose(tile[:, :HD])
                values_ref[pl.ds(at, BLK), :] = tile[:, HD:]


def stacked(tile):
    heads = tile.shape[1] // HD
    return jnp.concatenate([tile[:, i * HD : (i + 1) * HD] for i in range(heads)], axis=0)


def load_rows(query_from, grad_from, saved_from, q_ref, g_ref, dots_ref):
    lane = lax.broadcasted_iota(jnp.int32, (BLK, HD), 1)
    dots = jnp.zeros((BLK, HD), F32)
    for h in range(STEP // HD):
        columns = slice(h * HD, (h + 1) * HD)
        rows = slice(h * BLK, (h + 1) * BLK)
        grad = grad_from[:, columns]
        q_ref[rows, :] = query_from[:, columns]
        g_ref[rows, :] = grad
        product = grad.astype(F32) * saved_from[:, columns].astype(F32)
        dots = jnp.where(lane == h, jnp.sum(product, axis=1, keepdims=True), dots)
    dots_ref[...] = jnp.transpose(dots)


def block_pairs(size, start, key_ref, turned_ref, value_ref, q_ref, g_ref, dots_ref, dq_ref, dk_ref, dv_ref):
    rows = size * BLK
    first = pl.multiple_of(start * BLK, BLK)
    keys = key_ref[pl.ds(first, rows), :]
    values = value_ref[pl.ds(first, rows), :]
    keys_turned = turned_ref[:, pl.ds(first, rows)]
    wide = 2 * HD
    key_index = lax.broadcasted_iota(jnp.int32, (BLK, wide), 0)
    query_index = lax.broadcasted_iota(jnp.int32, (BLK, wide), 1) % BLK
    dk = None
    dv = None
    for part in range(STEP // wide):
        query = q_ref[part * wide : (part + 1) * wide, :]
        grad = g_ref[part * wide : (part + 1) * wide, :]
        scores = lax.dot_general(keys, query, NT, preferred_element_type=F32)
        dprobs = lax.dot_general(values, grad, NT, preferred_element_type=F32)
        row_dots = jnp.concatenate([dots_ref[part * 2 + i : part * 2 + i + 1, :] for i in range(2)], axis=1)
        last = jnp.where(key_index <= query_index, scores[rows - BLK :], -jnp.inf)
        scores = last if size == 1 else jnp.concatenate([scores[: rows - BLK], last], axis=0)
        top = jnp.max(scores, axis=0, keepdims=True)
        weights = jnp.exp2((scores - top) * INVERSE2)
        total = jnp.sum(weights, axis=0, keepdims=True)
        probs = weights * (1.0 / total)
        dscores = (probs * (dprobs - row_dots)).astype(BF16)
        dv_part = jnp.dot(probs.astype(BF16), grad, preferred_element_type=F32)
        dk_part = jnp.dot(dscores, query, preferred_element_type=F32)
        dv = dv_part if dv is None else dv + dv_part
        dk = dk_part if dk is None else dk + dk_part
        dq = jnp.dot(keys_turned, dscores, preferred_element_type=F32) * INVERSE
        for i in range(2):
            at = part * wide + i * HD
            dq_ref[:, at : at + HD] = jnp.transpose(dq[:, i * HD : (i + 1) * HD]).astype(BF16)
    dv_ref[pl.ds(first, rows), :] += dv
    dk_ref[pl.ds(first, rows), :] += dk


def rows_kernel(rows_of, place_ref, order_ref, docs_ref, key_ref, turned_ref, value_ref, query_ref, grad_ref, saved_ref, *refs):
    refs = list(refs)
    before_ref = refs.pop(0) if rows_of else None
    dq_ref = refs.pop(0)
    out_refs = [refs.pop(0) for _ in range(4 if rows_of else 1)]
    q_scr, g_scr, dots_scr, *rest = refs
    sums_ref = rest.pop(0) if rows_of else out_refs[0]
    step = pl.program_id(0)
    block = pl.program_id(1)

    @pl.when((step == 0) & (block == 0))
    def _():
        if rows_of:
            pltpu.make_async_copy(before_ref, rest[0], rest[1]).start()
        sums_ref[...] = jnp.zeros_like(sums_ref)

    load_rows(query_ref, grad_ref, saved_ref, q_scr, g_scr, dots_scr)
    core = 1 - place_ref[1] if rows_of else place_ref[1]
    seq = order_ref[place_ref[0] * 4 + core * 2 + block]
    doc = docs_ref[seq]
    start = jnp.int32(0)
    for b in range(BLOCKS):
        start = start + jnp.where(docs_ref[b] < doc, 1, 0)
    size = seq + 1 - start
    for i in range(1, LONGEST + 1):

        @pl.when(size == i)
        def _():
            block_pairs(
                i, start, key_ref, turned_ref, value_ref, q_scr, g_scr, dots_scr, dq_ref, sums_ref.at[0], sums_ref.at[1]
            )

    if rows_of:

        @pl.when((step == STEPS - 1) & (block == 1))
        def _():
            pltpu.make_async_copy(before_ref, rest[0], rest[1]).wait()
            for d in range(4):
                out_ref = out_refs[d]
                for r in range(4):
                    core_to = place_ref[1] if r < 2 else 1 - place_ref[1]
                    tp_to = place_ref[2] if r % 2 == 0 else 1 - place_ref[2]
                    stored = lax.rem(place_ref[0] + d, 4) * 4 + core_to * 2 + tp_to
                    at = pl.ds(pl.multiple_of(order_ref[stored] * BLK, BLK), BLK)
                    dk = (sums_ref[0, at, :] + rest[0][0, at, :]) * INVERSE
                    dv = sums_ref[1, at, :] + rest[0][1, at, :]
                    out_ref[r, :, :HD] = dk.astype(out_ref.dtype)
                    out_ref[r, :, HD:] = dv.astype(out_ref.dtype)


def rows_call(rows_of, place, order, docs, kv, queries, saved, grads, sums):
    whole = lambda s: pl.BlockSpec(s, lambda i, j, *_: (0,) * len(s))
    group_at = pl.BlockSpec((BLK, STEP), lambda i, j, p, *_: (j, p[1] * STEPS + i))
    alone_at = pl.BlockSpec((BLK, STEP), lambda i, j, *_: (j, i))
    sums_shape = (2, TOKENS, HD)
    in_specs = [whole((TOKENS, HD)), whole((HD, TOKENS)), whole((TOKENS, HD)), group_at, alone_at, group_at]
    operands = [*kv, queries, grads, saved]
    scratch = [pltpu.VMEM((STEP, HD), BF16), pltpu.VMEM((STEP, HD), BF16), pltpu.VMEM((HD, BLK), F32)]
    if rows_of:
        in_specs.append(ANY)
        operands.append(sums)
        outs = [shape(ROWS, GROUP)] + [shape(4, BLK, 2 * HD, dtype=BF16 if d else F32) for d in range(4)]
        scratch += [pltpu.VMEM(sums_shape, F32), pltpu.VMEM(sums_shape, F32), pltpu.SemaphoreType.DMA]
    else:
        outs = [shape(*queries.shape), shape(*sums_shape, dtype=F32)]
    return pl.pallas_call(
        functools.partial(rows_kernel, rows_of),
        grid_spec=pltpu.PrefetchScalarGridSpec(
            num_scalar_prefetch=3,
            grid=(STEPS, 2),
            in_specs=in_specs,
            out_specs=[alone_at if rows_of else group_at] + [whole(out.shape) for out in outs[1:]],
            scratch_shapes=scratch,
        ),
        out_shape=outs,
        compiler_params=pltpu.CompilerParams(vmem_limit_bytes=62 << 20),
        cost_estimate=TINY,
    )(place, order, docs, *operands)


def place_kernel(place_ref, piece_ref, _, out_ref):
    out_ref[...] = piece_ref[...]


def on_device(queries, key_codes, value_codes, kv_scales, saved_out, section_grads, block_order, block_docs):
    ctx = lax.axis_index("ctx")
    core = ctx % 2
    place = jnp.stack([ctx // 2, core, lax.axis_index("tp")]).astype(jnp.int32)
    queries, saved_out, section_grads = queries[0], saved_out[0], section_grads[0]

    grads = []
    for flip in range(2):
        group = core if flip == 0 else 1 - core
        piece = lax.dynamic_slice_in_dim(section_grads, group * GROUP, GROUP, 1)
        grads.append(from_next_section(piece, flip))

    keep, send = pl.pallas_call(
        dequantize_kernel,
        in_specs=[SMEM, VMEM, VMEM, SMEM],
        out_specs=[VMEM] * 2,
        out_shape=[shape(ROWS, 2 * HD)] * 2,
        cost_estimate=TINY,
    )(place, key_codes[0], value_codes[0], kv_scales[0])
    sent = [core_swap(array) for array in (queries, saved_out)]
    chip = tied(jnp.stack([keep, core_swap(send)]), *sent)
    chips = [chip] + [chip_turned(chip, d) for d in range(1, 4)]
    kv = pl.pallas_call(
        order_kernel,
        in_specs=[SMEM, SMEM] + [VMEM] * 4,
        out_specs=[VMEM] * 3,
        out_shape=[shape(TOKENS, HD), shape(HD, TOKENS), shape(TOKENS, HD)],
        compiler_params=pltpu.CompilerParams(vmem_limit_bytes=62 << 20),
        cost_estimate=TINY,
    )(place, block_order, *chips)

    shared = (place, block_order, block_docs, kv)
    dq, sums = rows_call(0, *shared, queries, saved_out, grads[0], None)
    dq_other, own, *further = rows_call(1, *shared, *sent, grads[1], sums)
    returned = core_swap(dq_other)
    arrived = [chip_turned(part, d + 1) for d, part in enumerate(further)]
    dq = pl.pallas_call(
        place_kernel,
        grid_spec=pltpu.PrefetchScalarGridSpec(
            num_scalar_prefetch=1,
            grid=(4,),
            in_specs=[pl.BlockSpec((BLK // 2, GROUP), lambda i, p: (i, 0)), ANY],
            out_specs=pl.BlockSpec((BLK // 2, GROUP), lambda i, p: (i, 1 - p[1])),
        ),
        out_shape=shape(*queries.shape),
        input_output_aliases={2: 0},
        cost_estimate=TINY,
    )(place, returned, dq)
    arrived[1] = tied(arrived[1], dq)
    total = (own + sum(part.astype(F32) for part in arrived)).astype(BF16)
    tp = place[2]
    pieces = [total[0], turned(total[1], "tp"), core_swap(total[2]), across(total[3])]
    outs = []
    for part in range(2):
        columns = []
        for head in range(KVH):
            same_tp, same_core = tp == head // 2, core == head % 2
            near, apart = (
                jnp.where(same_tp, pieces[2 * i], pieces[2 * i + 1])[:, part * HD : (part + 1) * HD] for i in range(2)
            )
            columns.append(jnp.where(same_core, near, apart))
        outs.append(jnp.concatenate(columns, axis=1))
    grad_keys, grad_values = outs
    return dq[None], grad_keys[None], grad_values[None]


def solution(mesh):
    in_specs = (
        P("pipe", "ctx", "tp"),
        P("pipe", "ctx", "tp"),
        P("pipe", "ctx", "tp"),
        P("pipe", "ctx", None),
        P("pipe", "ctx", "tp"),
        P("pipe", "ctx", "tp"),
        P(),
        P(),
    )
    out_specs = (
        P("pipe", "ctx", "tp"),
        P("pipe", ("ctx", "tp"), None),
        P("pipe", ("ctx", "tp"), None),
    )
    return jax.shard_map(on_device, mesh=mesh, in_specs=in_specs, out_specs=out_specs, check_vma=False)
```

```python
import functools
import math

import jax
import jax.numpy as jnp
from jax import lax
from jax.experimental import pallas as pl
from jax.experimental.pallas import tpu as pltpu
from jax.sharding import PartitionSpec as P

HQ = 64
KVH = 4
HD = 128
BLK = 128
BLOCKS = 16
TOKENS = BLOCKS * BLK
ROWS = 2 * BLK
LONGEST = 9
INVERSE = HD**-0.5
INVERSE2 = INVERSE * math.log2(math.e)
NT = (((1,), (1,)), ((), ()))
F32 = jnp.float32
BF16 = jnp.bfloat16

GROUP = HQ // KVH * HD
STEP = 512
STEPS = GROUP // STEP
RING = 4
DIRECT = GROUP - STEP
SMEM = pl.BlockSpec(memory_space=pltpu.SMEM)
VMEM = pl.BlockSpec(memory_space=pltpu.VMEM)
ANY = pl.BlockSpec(memory_space=pl.ANY)
TINY = pl.CostEstimate(flops=1_000_000, bytes_accessed=100_000, transcendentals=0)


def shape(*dims, dtype=BF16):
    return jax.ShapeDtypeStruct(dims, dtype)


def chip_turned(array, by):
    size = lax.axis_size("ctx")
    return lax.ppermute(array, "ctx", [(i, (i + 2 * by) % size) for i in range(size)])


def turned(array, axis):
    size = lax.axis_size(axis)
    return lax.ppermute(array, axis, [(i, (i + 1) % size) for i in range(size)])


def across(array):
    size = lax.axis_size("ctx")
    moves = [(i * 2 + t, (i ^ 1) * 2 + 1 - t) for i in range(size) for t in range(2)]
    return lax.ppermute(array, ("ctx", "tp"), moves)


def core_swap(array):
    size = lax.axis_size("ctx")
    return lax.ppermute(array, "ctx", [(i, i ^ 1) for i in range(size)])


def from_next_section(array, flip):
    sections, size = lax.axis_size("pipe"), lax.axis_size("ctx")
    moves = [
        (s * size + i, (s - 1) % sections * size + (i ^ flip)) for s in range(sections) for i in range(size)
    ]
    return lax.ppermute(array, ("pipe", "ctx"), moves)


def long_way(array, hop):
    sections, size = lax.axis_size("pipe"), lax.axis_size("ctx")
    moves = []
    for s in range(sections):
        ring, at = s // RING, s % RING
        if hop == 0 and at == 0:
            ring = (ring - 1) % (sections // RING)
        target = ring * RING + (at + 1) % RING
        moves += [(s * size + i, target * size + (i ^ 1 if hop == RING - 2 else i)) for i in range(size)]
    return lax.ppermute(array, ("pipe", "ctx"), moves)


def tied(array, *others):
    return lax.optimization_barrier((array,) + others)[0]


def dequantize_kernel(place_ref, key_ref, value_ref, scale_ref, keep_ref, send_ref):
    core = place_ref[1]
    for g in range(2):
        for block in range(2):
            rows = slice(block * BLK, (block + 1) * BLK)
            for part, codes in enumerate((key_ref, value_ref)):
                scale = scale_ref[block, part * KVH + place_ref[2] * 2 + g]
                tile = (codes[rows, g * HD : (g + 1) * HD].astype(F32) * scale).astype(BF16)

                @pl.when(core == g)
                def _():
                    keep_ref[rows, part * HD : (part + 1) * HD] = tile

                @pl.when(core != g)
                def _():
                    send_ref[rows, part * HD : (part + 1) * HD] = tile


def order_kernel(place_ref, order_ref, *refs):
    pieces = refs[:4]
    keys_ref, turned_ref, values_ref = refs[4:]
    y = place_ref[0]
    for d in range(4):
        from_y = lax.rem(y + 4 - d, 4)
        for half in range(2):
            holder = jnp.where(half == 0, place_ref[1], 1 - place_ref[1])
            for block in range(2):
                seq = order_ref[from_y * 4 + holder * 2 + block]
                at = pl.multiple_of(seq * BLK, BLK)
                tile = pieces[d][half, block * BLK : (block + 1) * BLK, :]
                keys_ref[pl.ds(at, BLK), :] = tile[:, :HD]
                turned_ref[:, pl.ds(at, BLK)] = jnp.transpose(tile[:, :HD])
                values_ref[pl.ds(at, BLK), :] = tile[:, HD:]


def stacked(tile):
    heads = tile.shape[1] // HD
    return jnp.concatenate([tile[:, i * HD : (i + 1) * HD] for i in range(heads)], axis=0)


def load_rows(query_from, grad_from, saved_from, q_ref, g_ref, dots_ref):
    lane = lax.broadcasted_iota(jnp.int32, (BLK, HD), 1)
    dots = jnp.zeros((BLK, HD), F32)
    for h in range(STEP // HD):
        columns = slice(h * HD, (h + 1) * HD)
        rows = slice(h * BLK, (h + 1) * BLK)
        grad = grad_from[:, columns]
        q_ref[rows, :] = query_from[:, columns]
        g_ref[rows, :] = grad
        product = grad.astype(F32) * saved_from[:, columns].astype(F32)
        dots = jnp.where(lane == h, jnp.sum(product, axis=1, keepdims=True), dots)
    dots_ref[...] = jnp.transpose(dots)


def block_pairs(size, start, key_ref, turned_ref, value_ref, q_ref, g_ref, dots_ref, dq_ref, dk_ref, dv_ref):
    rows = size * BLK
    first = pl.multiple_of(start * BLK, BLK)
    keys = key_ref[pl.ds(first, rows), :]
    values = value_ref[pl.ds(first, rows), :]
    keys_turned = turned_ref[:, pl.ds(first, rows)]
    wide = 2 * HD
    key_index = lax.broadcasted_iota(jnp.int32, (BLK, wide), 0)
    query_index = lax.broadcasted_iota(jnp.int32, (BLK, wide), 1) % BLK
    dk = None
    dv = None
    for part in range(STEP // wide):
        query = q_ref[part * wide : (part + 1) * wide, :]
        grad = g_ref[part * wide : (part + 1) * wide, :]
        scores = lax.dot_general(keys, query, NT, preferred_element_type=F32)
        dprobs = lax.dot_general(values, grad, NT, preferred_element_type=F32)
        row_dots = jnp.concatenate([dots_ref[part * 2 + i : part * 2 + i + 1, :] for i in range(2)], axis=1)
        last = jnp.where(key_index <= query_index, scores[rows - BLK :], -jnp.inf)
        scores = last if size == 1 else jnp.concatenate([scores[: rows - BLK], last], axis=0)
        top = jnp.max(scores, axis=0, keepdims=True)
        weights = jnp.exp2((scores - top) * INVERSE2)
        total = jnp.sum(weights, axis=0, keepdims=True)
        probs = weights * (1.0 / total)
        dscores = (probs * (dprobs - row_dots)).astype(BF16)
        dv_part = jnp.dot(probs.astype(BF16), grad, preferred_element_type=F32)
        dk_part = jnp.dot(dscores, query, preferred_element_type=F32)
        dv = dv_part if dv is None else dv + dv_part
        dk = dk_part if dk is None else dk + dk_part
        dq = jnp.dot(keys_turned, dscores, preferred_element_type=F32) * INVERSE
        for i in range(2):
            at = part * wide + i * HD
            dq_ref[:, at : at + HD] = jnp.transpose(dq[:, i * HD : (i + 1) * HD]).astype(BF16)
    dv_ref[pl.ds(first, rows), :] += dv
    dk_ref[pl.ds(first, rows), :] += dk


def rows_kernel(rows_of, place_ref, order_ref, docs_ref, key_ref, turned_ref, value_ref, query_ref, saved_ref, grad_ref, *refs):
    refs = list(refs)
    around_ref = refs.pop(0) if rows_of else None
    before_ref = refs.pop(0) if rows_of else None
    dq_ref = refs.pop(0)
    out_refs = [refs.pop(0) for _ in range(4 if rows_of else 1)]
    q_scr, g_scr, dots_scr, *rest = refs
    sums_ref = rest.pop(0) if rows_of else out_refs[0]
    step = pl.program_id(0)
    block = pl.program_id(1)

    @pl.when((step == 0) & (block == 0))
    def _():
        if rows_of:
            pltpu.make_async_copy(before_ref, rest[0], rest[1]).start()
        sums_ref[...] = jnp.zeros_like(sums_ref)

    if rows_of:

        @pl.when(step < DIRECT // STEP)
        def _():
            load_rows(query_ref, grad_ref, saved_ref, q_scr, g_scr, dots_scr)

        @pl.when(step >= DIRECT // STEP)
        def _():
            load_rows(query_ref, around_ref, saved_ref, q_scr, g_scr, dots_scr)

    else:
        load_rows(query_ref, grad_ref, saved_ref, q_scr, g_scr, dots_scr)
    core = 1 - place_ref[1] if rows_of else place_ref[1]
    seq = order_ref[place_ref[0] * 4 + core * 2 + block]
    doc = docs_ref[seq]
    start = jnp.int32(0)
    for b in range(BLOCKS):
        start = start + jnp.where(docs_ref[b] < doc, 1, 0)
    size = seq + 1 - start
    for i in range(1, LONGEST + 1):

        @pl.when(size == i)
        def _():
            block_pairs(
                i, start, key_ref, turned_ref, value_ref, q_scr, g_scr, dots_scr, dq_ref, sums_ref.at[0], sums_ref.at[1]
            )

    if rows_of:

        @pl.when((step == STEPS - 1) & (block == 1))
        def _():
            pltpu.make_async_copy(before_ref, rest[0], rest[1]).wait()
            for d in range(4):
                out_ref = out_refs[d]
                for r in range(4):
                    core_to = place_ref[1] if r < 2 else 1 - place_ref[1]
                    tp_to = place_ref[2] if r % 2 == 0 else 1 - place_ref[2]
                    stored = lax.rem(place_ref[0] + d, 4) * 4 + core_to * 2 + tp_to
                    at = pl.ds(pl.multiple_of(order_ref[stored] * BLK, BLK), BLK)
                    dk = (sums_ref[0, at, :] + rest[0][0, at, :]) * INVERSE
                    dv = sums_ref[1, at, :] + rest[0][1, at, :]
                    out_ref[r, :, :HD] = dk.astype(out_ref.dtype)
                    out_ref[r, :, HD:] = dv.astype(out_ref.dtype)


def rows_call(rows_of, place, order, docs, kv, queries, saved, grads, sums):
    whole = lambda s: pl.BlockSpec(s, lambda i, j, *_: (0,) * len(s))
    group_at = pl.BlockSpec((BLK, STEP), lambda i, j, p, *_: (j, p[1] * STEPS + i))
    alone_at = pl.BlockSpec((BLK, STEP), lambda i, j, *_: (j, i))
    sums_shape = (2, TOKENS, HD)
    in_specs = [whole((TOKENS, HD)), whole((HD, TOKENS)), whole((TOKENS, HD)), group_at, group_at]
    operands = [*kv, queries, saved, *grads]
    if rows_of:
        in_specs.append(pl.BlockSpec((BLK, STEP), lambda i, j, *_: (j, jnp.minimum(i, DIRECT // STEP - 1))))
        in_specs.append(pl.BlockSpec((BLK, STEP), lambda i, j, *_: (j, jnp.maximum(i - DIRECT // STEP, 0))))
    else:
        in_specs.append(alone_at)
    scratch = [pltpu.VMEM((STEP, HD), BF16), pltpu.VMEM((STEP, HD), BF16), pltpu.VMEM((HD, BLK), F32)]
    if rows_of:
        in_specs.append(ANY)
        operands.append(sums)
        outs = [shape(ROWS, GROUP)] + [shape(4, BLK, 2 * HD, dtype=BF16 if d else F32) for d in range(4)]
        scratch += [pltpu.VMEM(sums_shape, F32), pltpu.VMEM(sums_shape, F32), pltpu.SemaphoreType.DMA]
    else:
        outs = [shape(*queries.shape), shape(*sums_shape, dtype=F32)]
    return pl.pallas_call(
        functools.partial(rows_kernel, rows_of),
        grid_spec=pltpu.PrefetchScalarGridSpec(
            num_scalar_prefetch=3,
            grid=(STEPS, 2),
            in_specs=in_specs,
            out_specs=[alone_at if rows_of else group_at] + [whole(out.shape) for out in outs[1:]],
            scratch_shapes=scratch,
        ),
        out_shape=outs,
        compiler_params=pltpu.CompilerParams(vmem_limit_bytes=62 << 20),
        cost_estimate=TINY,
    )(place, order, docs, *operands)


def place_kernel(place_ref, piece_ref, _, out_ref):
    out_ref[...] = piece_ref[...]


def on_device(queries, key_codes, value_codes, kv_scales, saved_out, section_grads, block_order, block_docs):
    ctx = lax.axis_index("ctx")
    core = ctx % 2
    place = jnp.stack([ctx // 2, core, lax.axis_index("tp")]).astype(jnp.int32)
    queries, saved_out, section_grads = queries[0], saved_out[0], section_grads[0]

    first = (1 - core) * GROUP
    own_rows = lax.dynamic_slice_in_dim(section_grads, core * GROUP, GROUP, 1)
    direct = lax.dynamic_slice_in_dim(section_grads, first, DIRECT, 1)
    around = lax.dynamic_slice_in_dim(section_grads, first + DIRECT, GROUP - DIRECT, 1)
    key_codes = tied(key_codes, own_rows, direct, around)
    own_rows = from_next_section(own_rows, 0)
    direct = from_next_section(direct, 1)
    around = long_way(around, 0)

    keep, send = pl.pallas_call(
        dequantize_kernel,
        in_specs=[SMEM, VMEM, VMEM, SMEM],
        out_specs=[VMEM] * 2,
        out_shape=[shape(ROWS, 2 * HD)] * 2,
        cost_estimate=TINY,
    )(place, key_codes[0], value_codes[0], kv_scales[0])
    sent = [core_swap(array) for array in (queries, saved_out)]
    chip = tied(jnp.stack([keep, core_swap(send)]), *sent)
    chips = [chip] + [chip_turned(chip, d) for d in range(1, 4)]
    around = long_way(tied(around, chips[2]), 1)
    around = long_way(around, 2)
    kv = pl.pallas_call(
        order_kernel,
        in_specs=[SMEM, SMEM] + [VMEM] * 4,
        out_specs=[VMEM] * 3,
        out_shape=[shape(TOKENS, HD), shape(HD, TOKENS), shape(TOKENS, HD)],
        compiler_params=pltpu.CompilerParams(vmem_limit_bytes=62 << 20),
        cost_estimate=TINY,
    )(place, block_order, *chips)

    shared = (place, block_order, block_docs, kv)
    dq, sums = rows_call(0, *shared, queries, saved_out, [own_rows], None)
    dq_other, own, *further = rows_call(1, *shared, *sent, [direct, around], sums)
    returned = core_swap(dq_other)
    arrived = [chip_turned(part, d + 1) for d, part in enumerate(further)]
    dq = pl.pallas_call(
        place_kernel,
        grid_spec=pltpu.PrefetchScalarGridSpec(
            num_scalar_prefetch=1,
            grid=(4,),
            in_specs=[pl.BlockSpec((BLK // 2, GROUP), lambda i, p: (i, 0)), ANY],
            out_specs=pl.BlockSpec((BLK // 2, GROUP), lambda i, p: (i, 1 - p[1])),
        ),
        out_shape=shape(*queries.shape),
        input_output_aliases={2: 0},
        cost_estimate=TINY,
    )(place, returned, dq)
    arrived[1] = tied(arrived[1], dq)
    total = (own + sum(part.astype(F32) for part in arrived)).astype(BF16)
    tp = place[2]
    pieces = [total[0], turned(total[1], "tp"), core_swap(total[2]), across(total[3])]
    outs = []
    for part in range(2):
        columns = []
        for head in range(KVH):
            same_tp, same_core = tp == head // 2, core == head % 2
            near, apart = (
                jnp.where(same_tp, pieces[2 * i], pieces[2 * i + 1])[:, part * HD : (part + 1) * HD] for i in range(2)
            )
            columns.append(jnp.where(same_core, near, apart))
        outs.append(jnp.concatenate(columns, axis=1))
    grad_keys, grad_values = outs
    return dq[None], grad_keys[None], grad_values[None]


def solution(mesh):
    in_specs = (
        P("pipe", "ctx", "tp"),
        P("pipe", "ctx", "tp"),
        P("pipe", "ctx", "tp"),
        P("pipe", "ctx", None),
        P("pipe", "ctx", "tp"),
        P("pipe", "ctx", "tp"),
        P(),
        P(),
    )
    out_specs = (
        P("pipe", "ctx", "tp"),
        P("pipe", ("ctx", "tp"), None),
        P("pipe", ("ctx", "tp"), None),
    )
    return jax.shard_map(on_device, mesh=mesh, in_specs=in_specs, out_specs=out_specs, check_vma=False)
```
